256 devices in a mesh: band: 32 (over y, z_lo, core), grid: 8 (over z_hi, x).
Axes of the slice: x: 4, y: 4, z: 8 (z_hi: 2, z_lo: 4; z = z_hi * 4 + z_lo), core: 2. Of those that a mesh axis runs over, the one named last changes fastest.
Arguments:
- occ_orbitals: bfloat16 [32, 128, 128, 128], P('band', 'grid'), may hold values from -6 to 6
- occ_mask: int32 [32], P('band'), may hold values 0 or 1
- resp_orbitals: bfloat16 [96, 128, 128, 128], P('band', 'grid'), may hold values from -6 to 6
- kernel_index: int32 [128, 128, 128], P(None, 'grid'), may hold values from 0 to 31, as said below
- kernel_table: float32 [32], replicated, may hold values from 0.05 to 2
Outputs:
- occ_potential: bfloat16 [32, 128, 128, 128], P('band', 'grid')
- resp_potential: bfloat16 [96, 128, 128, 128], P('band', 'grid')
The draws below stay inside these ranges and needn't reach their ends.
Inputs may be any that keep to these rules, and one draw needn't show every extreme that they name: kernel_index[a, b, c] is unchanged when a is replaced by (128 - a) mod 128, and likewise for b and for c.
All inputs are finite; a program needn't handle non-finite values. No bound on the sum of `occ_mask` on one device may be relied on, other than what follows from the above.
Results may differ from the reference program's by a relative error of at most 0.0042.
Values may be sent and summed in bfloat16 or wider, within the bound.
No kernel may reach another device: no remote copies, remote signals or barrier semaphores. Data moves between devices by JAX's collectives and lax.ppermute only.
A program may use at most 128 MiB of HBM per device.

```python
import math
import jax
import jax.numpy as jnp
from jax import lax

N = 128
KT = 32
OCC_DEV = 1
RESP_DEV = 3
STEPS = 4
NOCC = 32
NRESP = 96
N_BAND = 32


def draw_kernel_index(key, part):
    key = jax.random.fold_in(key, 11)
    octant_size = N // 2 + 1
    octant = jax.random.randint(key, (octant_size, octant_size, octant_size), 0, KT, dtype=jnp.int32)
    octant = octant.at[0, 0, 0].set(KT - 1)
    octant = octant.at[1, 1, 1].set(0)
    counter = jnp.arange(N, dtype=jnp.int32)
    folded = jnp.minimum(counter, N - counter)
    return octant[folded][:, folded][:, :, folded]


def touch_ends(values, stream_key, low, top_value):
    longest = values.shape.index(max(values.shape))
    spots = []
    for shift in (0, 1):
        where = [jax.random.randint(jax.random.fold_in(stream_key, axis), (), 0, length) for axis, length in enumerate(values.shape)]
        where[longest] = (where[longest] + shift) % values.shape[longest]
        spots.append(tuple(where))
    return values.at[spots[0]].set(low).at[spots[1]].set(top_value)


def block_levels(key, dims, shards, low, largest):
    loudness, own = 1.0, jax.random.fold_in(key, 6)
    for dim, shards_of in shards:
        steps = jnp.exp(jax.random.uniform(jax.random.fold_in(own, dim), (shards_of,), jnp.float32, low / len(shards), largest / len(shards)))
        loudness = loudness * jnp.repeat(steps, dims[dim] // shards_of).reshape([-1 if axis == dim else 1 for axis in range(len(dims))])
    return loudness


def bell_draw(key, extent, spread, bound, split=(), held_as=jnp.bfloat16):
    result = jax.random.normal(key, extent, jnp.float32) * spread
    if len(split) > 0:
        result = block_levels(key, extent, split, -0.22, 0.18) * result
    return jnp.clip(result, min=-bound, max=bound).astype(held_as)


def setup_inputs(seed: int = 0) -> dict:
    seeds = jax.random.split(jax.random.key(seed), 6)
    return {
        "occ_orbitals": bell_draw(seeds[0], (NOCC, N, N, N), 1.0, 6.0, ((0, 32), (1, 8))),
        "occ_mask": touch_ends((jax.random.randint(seeds[1], (NOCC,), 0, 4) < 3).astype(jnp.int32), jax.random.fold_in(seeds[1], 1), 0, 1),
        "resp_orbitals": bell_draw(seeds[2], (NRESP, N, N, N), 1.0, 6.0, ((0, 32), (1, 8))),
        "kernel_index": draw_kernel_index(jax.random.fold_in(seeds[5], 71), 0),
        "kernel_table": jnp.clip(jnp.exp(jax.random.uniform(seeds[4], (KT,), jnp.float32, math.log(0.05), math.log(2.0))), 0.05, 2.0),
    }


HIGHEST = lax.Precision.HIGHEST


def cas_matrix(length):
    counter = jnp.arange(length, dtype=jnp.int32)
    product = (counter[:, None] * counter[None, :]) % length
    angles = (2.0 * math.pi / length) * product.astype(jnp.float32)
    return jnp.cos(angles) + jnp.sin(angles)


def inner_pair(field, cas_table):
    along_last = jnp.einsum('abc,kc->abk', field, cas_table, precision=HIGHEST)
    return jnp.einsum('abk,jb->ajk', along_last, cas_table, precision=HIGHEST)


def pair_field(density, cas_table, kernel):
    half_form = inner_pair(density, cas_table).astype(jnp.bfloat16)
    half_form = lax.optimization_barrier(half_form).astype(jnp.float32)
    spectrum = jnp.einsum('abk,ia->ibk', half_form, cas_table, precision=HIGHEST) * kernel
    mixed = jnp.einsum('ibk,ia->abk', spectrum, cas_table, precision=HIGHEST).astype(jnp.bfloat16)
    mixed = lax.optimization_barrier(mixed).astype(jnp.float32)
    return inner_pair(mixed, cas_table) / float(N ** 3)


def reference(occ_orbitals, occ_mask, resp_orbitals, kernel_index, kernel_table):
    cas_table = cas_matrix(N)
    kernel = kernel_table[kernel_index]
    occupied = occ_orbitals * occ_mask.astype(jnp.bfloat16)[:, None, None, None]
    occ_start = jnp.zeros((NOCC, N, N, N), jnp.float32)
    resp_start = jnp.zeros((NRESP, N, N, N), jnp.float32)

    def per_response(orbital_index, carry):
        occ_sums, resp_sums = carry
        orbital_index = jnp.asarray(orbital_index).astype(jnp.int32)
        block = orbital_index // RESP_DEV
        response = lax.dynamic_index_in_dim(resp_orbitals, orbital_index, 0, keepdims=False).astype(jnp.float32)
        total = jnp.zeros((N, N, N), jnp.float32)
        for cycle_step in range(STEPS):
            for member in range(OCC_DEV):
                occ_index = (((block - cycle_step) % N_BAND) * OCC_DEV + member).astype(jnp.int32)
                orbital = lax.dynamic_index_in_dim(occupied, occ_index, 0, keepdims=False).astype(jnp.float32)
                potential = pair_field(orbital * response, cas_table, kernel)
                total = total + potential * orbital
                occ_sums = occ_sums.at[occ_index].add(potential * response)
        resp_sums = resp_sums.at[orbital_index].set(total)
        return occ_sums, resp_sums

    occ_sums, resp_sums = lax.fori_loop(0, NRESP, per_response, (occ_start, resp_start))
    return occ_sums.astype(jnp.bfloat16), resp_sums.astype(jnp.bfloat16)
```

```python
import math

import jax
import jax.numpy as jnp
from jax import lax
from jax.experimental import pallas as pl
from jax.experimental.pallas import tpu as pltpu
from jax.sharding import PartitionSpec as P

BF, F32 = jnp.bfloat16, jnp.float32
STEPS = 4
AXES = ("band", "grid")
NY, NZ, NX = 4, 4, 4
VMEM = 40 << 20


def flat(y, zl, c, h, x):
    return (y * NZ * 2 + zl * 2 + c) * (2 * NX) + h * NX + x


def route(move):
    return [
        (flat(y, zl, c, h, x), flat(*move(y, zl, c, h, x)))
        for y in range(NY)
        for zl in range(NZ)
        for c in range(2)
        for h in range(2)
        for x in range(NX)
    ]


def place(y, c):
    return NY - 1 - y if c else y


def to_place(y, zl, c, h, x):
    return place(y, c), zl, c, h, x


def to_half(y, zl, c, h, x):
    return y, zl, h, c ^ (y // 2), x


def to_next(y, zl, c, h, x):
    core = (y // 2) ^ h
    q = (place(y, core) * NZ * 2 + zl * 2 + core + 1) % (NY * NZ * 2)
    y, zl, core = q // (2 * NZ), q // 2 % NZ, q % 2
    return place(y, core), zl, c, y // 2, x


def to_twin(y, zl, c, h, x):
    return y, zl, 1 - c, h, x


def to_mirror(y, zl, c, h, x):
    return y, zl, c, 1 - h, x


def along_x(distance):
    return lambda y, zl, c, h, x: (y, zl, c, h, (x + distance) % NX)


def send(block, move, back=False):
    pairs = route(move)
    return lax.ppermute(block, AXES, [(b, a) for a, b in pairs] if back else pairs)


def cas(rows, columns, length):
    product = (rows[:, None] * columns[None, :]) % length
    angles = (2.0 * math.pi / length) * product.astype(F32)
    return jnp.cos(angles) + jnp.sin(angles)


def halves(table, axis):
    high = lax.reduce_precision(table, 8, 7)
    return jnp.concatenate([high.astype(BF), (table - high).astype(BF)], axis=axis)


def dot(a, b):
    return jnp.dot(a, b, preferred_element_type=F32)


def twice(block, axis):
    return jnp.concatenate([block, block], axis=axis)


def lookup_body(index_ref, mirror_ref, table_ref, out_ref, extra_ref):
    n, slab, _ = extra_ref.shape[1], out_ref.shape[0], None
    table = jnp.broadcast_to(table_ref[...], (n, n))
    for b in range(slab):
        entry = index_ref[pl.ds(b, n, stride=slab), :]
        out_ref[b] = jnp.take_along_axis(table, entry, axis=1, mode="promise_in_bounds")
    extra_ref[0] = jnp.take_along_axis(table, mirror_ref[...], axis=1, mode="promise_in_bounds")


def lookup(index, mirror, table):
    n, slab, _ = index.shape
    row = jnp.zeros((1, n), F32).at[0, : table.shape[0]].set(table)
    return pl.pallas_call(
        lookup_body,
        out_shape=[jax.ShapeDtypeStruct((slab, n, n), F32), jax.ShapeDtypeStruct((1, n, n), F32)],
        compiler_params=pltpu.CompilerParams(vmem_limit_bytes=VMEM),
        cost_estimate=pl.CostEstimate(flops=0, bytes_accessed=8 << 20, transcendentals=0),
        name="lookup",
    )(index.reshape(n * slab, n), mirror, row)


def forward_body(occ0, occ1, resp0, resp1, right_ref, left_ref, *rest):
    outs, half_ref = rest[:-1], rest[-1]
    slab, n = occ0.shape[1], occ0.shape[3]
    per = n // len(outs)

    def part(occ_ref, resp_ref):
        density = (occ_ref[0] * resp_ref[0]).reshape(slab * n, n)
        along = dot(twice(density, 1), right_ref[...]).astype(BF)
        left = left_ref[...]
        for x in range(0, slab, 2):
            pair = jnp.concatenate([along[(x + i) * n : (x + i + 1) * n] for i in range(2)], axis=1)
            both = dot(left, twice(pair, 0))
            for i in range(2):
                half_ref[pl.ds((x + i) * n, n), :] = both[:, i * n : (i + 1) * n]
        for b in range(n):
            outs[b // per][b % per] = half_ref[pl.ds(b, slab, stride=n), :].astype(BF)

    @pl.when(pl.program_id(0) == 0)
    def _():
        part(occ0, resp0)

    @pl.when(pl.program_id(0) == 1)
    def _():
        part(occ1, resp1)


def forward(occ, resp, right, left):
    _, slab, n, _ = occ[0].shape
    per = n // NX
    whole = pl.BlockSpec((1, slab, n, n), lambda i: (0, 0, 0, 0))
    return pl.pallas_call(
        forward_body,
        grid=(2,),
        in_specs=[whole] * 4
        + [pl.BlockSpec(right.shape, lambda i: (0, 0)), pl.BlockSpec(left.shape, lambda i: (0, 0))],
        out_specs=[pl.BlockSpec((per, slab, n), lambda i: (0, i, 0))] * NX,
        out_shape=[jax.ShapeDtypeStruct((per, 2 * slab, n), BF)] * NX,
        scratch_shapes=[pltpu.VMEM((slab * n, n), F32)],
        compiler_params=pltpu.CompilerParams(vmem_limit_bytes=VMEM),
        cost_estimate=pl.CostEstimate(flops=0, bytes_accessed=12 << 20, transcendentals=0),
        name="forward",
    )(*occ, *resp, right, left)


def middle_body(p0, p1, p2, p3, kernel_ref, extra_ref, forth_ref, back_ref, *outs):
    ins = (p0, p1, p2, p3)
    rows, planes, n = p0.shape
    forth, back = forth_ref[...], back_ref[...]
    first = jnp.where(pl.program_id(0) == 0, kernel_ref[0], extra_ref[0])
    for b in range(0, rows, 2):
        field = jnp.concatenate(
            [jnp.concatenate([r[b + i] for r in ins], axis=0) for i in range(2)], axis=1
        )
        spectrum = dot(forth, twice(field, 0))
        weights = (first if b == 0 else kernel_ref[b], kernel_ref[b + 1])
        spectrum = jnp.concatenate(
            [(spectrum[:, i * n : (i + 1) * n] * weights[i]).astype(BF) for i in range(2)], axis=1
        )
        mixed = dot(back, twice(spectrum, 0)).astype(BF)
        for p, out in enumerate(outs):
            for i in range(2):
                out[b + i] = mixed[p * planes : (p + 1) * planes, i * n : (i + 1) * n]


def middle(pieces, kernel, extra, forth, back):
    rows, planes, n = pieces[0].shape
    slab = kernel.shape[0]
    piece = pl.BlockSpec((slab, planes, n), lambda i: (i, 0, 0))
    return pl.pallas_call(
        middle_body,
        grid=(rows // slab,),
        in_specs=[piece] * NX
        + [
            pl.BlockSpec(kernel.shape, lambda i: (0, 0, 0)),
            pl.BlockSpec(extra.shape, lambda i: (0, 0, 0)),
            pl.BlockSpec(forth.shape, lambda i: (0, 0)),
            pl.BlockSpec(back.shape, lambda i: (0, 0)),
        ],
        out_specs=[piece] * NX,
        out_shape=[jax.ShapeDtypeStruct((rows, planes, n), BF)] * NX,
        compiler_params=pltpu.CompilerParams(vmem_limit_bytes=VMEM),
        cost_estimate=pl.CostEstimate(flops=0, bytes_accessed=8 << 20, transcendentals=0),
        name="middle",
    )(*pieces, kernel, extra, forth, back)


def inverse_body(p0, p1, p2, p3, occ0, occ1, resp0, resp1, right_ref, left_ref, *rest):
    accumulators, (to0, to1, tr0, tr1, half_ref) = rest[:-5], rest[-5:]
    ins = (p0, p1, p2, p3)
    rows, slab, n = p0.shape
    part_rows = rows * slab

    def part(occ_ref, resp_ref, occ_out, resp_out, occ_in, resp_in):
        right, left = right_ref[...], left_ref[...]
        for p, piece in enumerate(ins):
            field = piece[...].reshape(part_rows, n)
            half_ref[pl.ds(p * part_rows, part_rows), :] = dot(twice(field, 1), right)
        for x in range(0, slab, 2):
            pair = jnp.concatenate(
                [half_ref[pl.ds(x + i, n, stride=slab), :].astype(BF) for i in range(2)], axis=1
            )
            both = dot(left, twice(pair, 0))
            for i in range(2):
                potential = both[:, i * n : (i + 1) * n]
                to_occ = potential * resp_ref[0, x + i].astype(F32)
                to_resp = potential * occ_ref[0, x + i].astype(F32)
                occ_out[0, x + i] = to_occ if occ_in is None else occ_in[0, x + i] + to_occ
                resp_out[0, x + i] = to_resp if resp_in is None else resp_in[0, x + i] + to_resp

    given = [None if a is None else a for a in accumulators]

    @pl.when(pl.program_id(0) == 0)
    def _():
        part(occ0, resp0, to0, tr0, given[0], given[2])

    @pl.when(pl.program_id(0) == 1)
    def _():
        part(occ1, resp1, to1, tr1, given[1], given[3])


def inverse(pieces, occ, resp, right, left, occ_sums, resp_sums):
    rows, planes, n = pieces[0].shape
    slab = planes // 2
    whole = pl.BlockSpec((1, slab, n, n), lambda i: (0, 0, 0, 0))
    sums = [*(occ_sums or (None, None)), *(resp_sums or (None, None))]
    present = [s for s in sums if s is not None]

    def body(*refs):
        refs = list(refs)
        head, tail = refs[:10], refs[10:]
        given = [None if s is None else tail.pop(0) for s in sums]
        inverse_body(*head, *given, *tail)

    return pl.pallas_call(
        body,
        grid=(2,),
        in_specs=[pl.BlockSpec((rows, slab, n), lambda i: (0, i, 0))] * NX
        + [whole] * 4
        + [pl.BlockSpec(right.shape, lambda i: (0, 0)), pl.BlockSpec(left.shape, lambda i: (0, 0))]
        + [whole] * len(present),
        out_specs=[whole] * 4,
        out_shape=[jax.ShapeDtypeStruct((1, slab, n, n), F32)] * 4,
        scratch_shapes=[pltpu.VMEM((slab * n, n), F32)],
        compiler_params=pltpu.CompilerParams(vmem_limit_bytes=VMEM),
        cost_estimate=pl.CostEstimate(flops=0, bytes_accessed=14 << 20, transcendentals=0),
        name="inverse",
    )(*pieces, *occ, *resp, right, left, *present)


def shards(occ_orbitals, occ_mask, resp_orbitals, kernel_index, kernel_table):
    n = occ_orbitals.shape[-1]
    slab = occ_orbitals.shape[1]
    responses = resp_orbitals.shape[0]
    band, grid = lax.axis_index("band"), lax.axis_index("grid")
    core, x, half = band % 2, grid % NX, grid // NX
    counter = jnp.arange(n, dtype=jnp.int32)

    own = jnp.arange(slab, dtype=jnp.int32)[None, :] + slab * (
        half * NX + (x + jnp.arange(NX, dtype=jnp.int32)) % NX
    )[:, None]
    mirrored = (n - own) % n
    mirrored = jnp.where(mirrored == own, (own + n // 2) % n, mirrored)
    frequencies = jnp.concatenate([own, mirrored], axis=1).reshape(-1)
    source = (x - jnp.arange(NX, dtype=jnp.int32)) % NX
    which = jnp.stack([core, 1 - core])
    planes = (
        which[None, :, None] * (NX * slab)
        + source[:, None, None] * slab
        + jnp.arange(slab, dtype=jnp.int32)[None, None, :]
    ).reshape(-1)
    straight = cas(counter, counter, n)
    right = halves(straight, 0)
    right_scaled = halves(straight * (1.0 / float(n**3)), 0)
    left = halves(cas(frequencies, counter, n), 1)
    left_back = halves(cas(counter, frequencies, n), 1)
    forth = halves(cas(counter, planes, n), 1)
    back = halves(cas(planes, counter, n), 1)

    edge = send(kernel_index[:, 0, :], to_mirror)
    edge = jnp.where(x == 0, edge, kernel_index[:, 0, :])
    kernel, extra = lookup(kernel_index, edge, kernel_table)

    occupied = occ_orbitals * occ_mask.astype(BF)[:, None, None, None]

    def gather(block):
        return send(send(block, to_place), to_half)

    def give_back(block):
        return send(send(block, to_half, back=True), to_place, back=True)

    occ = [gather(occupied)]
    resp = [gather(resp_orbitals[j : j + 1]) for j in range(responses)]
    for _ in range(STEPS - 1):
        occ.append(send(occ[-1], to_next))
    is_low = core == 0
    occ_pairs, resp_pairs = [], []
    for k in range(0, STEPS, 2):
        kept = jnp.where(is_low, occ[k], occ[k + 1])
        given = jnp.where(is_low, occ[k + 1], occ[k])
        occ_pairs.append((kept, send(given, to_twin)))
    for j in range(responses):
        resp_pairs.append((resp[j], send(resp[j], to_twin)))

    def spread(pieces, sign):
        return [pieces[0]] + [send(pieces[s], along_x(sign * s)) for s in range(1, NX)]

    order = [(0, 0)] + [(1, j) for j in range(responses)] + [(0, j) for j in range(1, responses)]
    occ_sums = [None] * (STEPS // 2)
    resp_sums = [None] * responses
    for k, j in order:
        pieces = forward(occ_pairs[k], resp_pairs[j], right, left)
        pieces = middle(spread(pieces, 1), kernel, extra, forth, back)
        o0, o1, r0, r1 = inverse(
            spread(pieces, -1), occ_pairs[k], resp_pairs[j], right_scaled, left_back, occ_sums[k], resp_sums[j]
        )
        occ_sums[k], resp_sums[j] = (o0, o1), (r0, r1)

    resp_out = []
    for j in range(responses):
        kept, given = resp_sums[j]
        total = kept + send(given, to_twin)
        resp_out.append(give_back(total.astype(BF)))

    by_step = [None] * STEPS
    for k in range(STEPS // 2):
        kept, given = occ_sums[k]
        other = send(given, to_twin)
        by_step[2 * k] = jnp.where(is_low, kept, other)
        by_step[2 * k + 1] = jnp.where(is_low, other, kept)
    total = by_step[-1]
    for s in reversed(range(STEPS - 1)):
        total = by_step[s] + send(total.astype(BF), to_next, back=True).astype(F32)
    return give_back(total.astype(BF)), jnp.concatenate(resp_out, axis=0)


def solution(mesh):
    in_specs = (
        P("band", "grid", None, None),
        P("band"),
        P("band", "grid", None, None),
        P(None, "grid", None),
        P(),
    )
    out_specs = (P("band", "grid", None, None), P("band", "grid", None, None))
    return jax.shard_map(shards, mesh=mesh, in_specs=in_specs, out_specs=out_specs, check_vma=False)
```

```python
import math

import jax
import jax.numpy as jnp
from jax import lax
from jax.experimental import pallas as pl
from jax.experimental.pallas import tpu as pltpu
from jax.sharding import PartitionSpec as P

BF, F32 = jnp.bfloat16, jnp.float32
STEPS = 4
AXES = ("band", "grid")
NY, NZ, NX = 4, 4, 4
VMEM = 40 << 20


def flat(y, zl, c, h, x):
    return (y * NZ * 2 + zl * 2 + c) * (2 * NX) + h * NX + x


def route(move):
    return [
        (flat(y, zl, c, h, x), flat(*move(y, zl, c, h, x)))
        for y in range(NY)
        for zl in range(NZ)
        for c in range(2)
        for h in range(2)
        for x in range(NX)
    ]


def place(y, c):
    return NY - 1 - y if c else y


def to_place(y, zl, c, h, x):
    return place(y, c), zl, c, h, x


def to_half(y, zl, c, h, x):
    return y, zl, h, c ^ (y // 2), x


def to_next(y, zl, c, h, x):
    core = (y // 2) ^ h
    q = (place(y, core) * NZ * 2 + zl * 2 + core + 1) % (NY * NZ * 2)
    y, zl, core = q // (2 * NZ), q // 2 % NZ, q % 2
    return place(y, core), zl, c, y // 2, x


def to_second(*at):
    return to_next(*to_next(*at))


def to_twin(y, zl, c, h, x):
    return y, zl, 1 - c, h, x


def to_mirror(y, zl, c, h, x):
    return y, zl, c, 1 - h, x


def along_x(distance):
    return lambda y, zl, c, h, x: (y, zl, c, h, (x + distance) % NX)


def send(block, move, back=False):
    pairs = route(move)
    return lax.ppermute(block, AXES, [(b, a) for a, b in pairs] if back else pairs)


def cas(rows, columns, length):
    product = (rows[:, None] * columns[None, :]) % length
    angles = (2.0 * math.pi / length) * product.astype(F32)
    return jnp.cos(angles) + jnp.sin(angles)


def halves(table, axis):
    high = lax.reduce_precision(table, 8, 7)
    return jnp.concatenate([high.astype(BF), (table - high).astype(BF)], axis=axis)


def dot(a, b):
    return jnp.dot(a, b, preferred_element_type=F32)


def twice(block, axis):
    return jnp.concatenate([block, block], axis=axis)


def lookup_body(index_ref, mirror_ref, table_ref, out_ref, extra_ref):
    n, slab, _ = extra_ref.shape[1], out_ref.shape[0], None
    table = jnp.broadcast_to(table_ref[...], (n, n))
    for b in range(slab):
        entry = index_ref[pl.ds(b, n, stride=slab), :]
        out_ref[b] = jnp.take_along_axis(table, entry, axis=1, mode="promise_in_bounds")
    extra_ref[0] = jnp.take_along_axis(table, mirror_ref[...], axis=1, mode="promise_in_bounds")


def lookup(index, mirror, table):
    n, slab, _ = index.shape
    row = jnp.zeros((1, n), F32).at[0, : table.shape[0]].set(table)
    return pl.pallas_call(
        lookup_body,
        out_shape=[jax.ShapeDtypeStruct((slab, n, n), F32), jax.ShapeDtypeStruct((1, n, n), F32)],
        compiler_params=pltpu.CompilerParams(vmem_limit_bytes=VMEM),
        cost_estimate=pl.CostEstimate(flops=0, bytes_accessed=8 << 20, transcendentals=0),
        name="lookup",
    )(index.reshape(n * slab, n), mirror, row)


def forward_body(occ0, occ1, resp0, resp1, right_ref, left_ref, *rest):
    outs, half_ref = rest[:-1], rest[-1]
    slab, n = occ0.shape[1], occ0.shape[3]
    per = n // len(outs)

    def part(occ_ref, resp_ref):
        density = (occ_ref[0] * resp_ref[0]).reshape(slab * n, n)
        along = dot(twice(density, 1), right_ref[...]).astype(BF)
        left = left_ref[...]
        for x in range(0, slab, 2):
            pair = jnp.concatenate([along[(x + i) * n : (x + i + 1) * n] for i in range(2)], axis=1)
            both = dot(left, twice(pair, 0))
            for i in range(2):
                half_ref[pl.ds((x + i) * n, n), :] = both[:, i * n : (i + 1) * n]
        for b in range(n):
            outs[b // per][b % per] = half_ref[pl.ds(b, slab, stride=n), :].astype(BF)

    @pl.when(pl.program_id(0) == 0)
    def _():
        part(occ0, resp0)

    @pl.when(pl.program_id(0) == 1)
    def _():
        part(occ1, resp1)


def forward(occ, resp, right, left):
    _, slab, n, _ = occ[0].shape
    per = n // NX
    whole = pl.BlockSpec((1, slab, n, n), lambda i: (0, 0, 0, 0))
    return pl.pallas_call(
        forward_body,
        grid=(2,),
        in_specs=[whole] * 4
        + [pl.BlockSpec(right.shape, lambda i: (0, 0)), pl.BlockSpec(left.shape, lambda i: (0, 0))],
        out_specs=[pl.BlockSpec((per, slab, n), lambda i: (0, i, 0))] * NX,
        out_shape=[jax.ShapeDtypeStruct((per, 2 * slab, n), BF)] * NX,
        scratch_shapes=[pltpu.VMEM((slab * n, n), F32)],
        compiler_params=pltpu.CompilerParams(vmem_limit_bytes=VMEM),
        cost_estimate=pl.CostEstimate(flops=0, bytes_accessed=12 << 20, transcendentals=0),
        name="forward",
    )(*occ, *resp, right, left)


def middle_body(p0, p1, p2, p3, kernel_ref, extra_ref, forth_ref, back_ref, *outs):
    ins = (p0, p1, p2, p3)
    rows, planes, n = p0.shape
    forth, back = forth_ref[...], back_ref[...]
    first = jnp.where(pl.program_id(0) == 0, kernel_ref[0], extra_ref[0])
    for b in range(0, rows, 2):
        field = jnp.concatenate(
            [jnp.concatenate([r[b + i] for r in ins], axis=0) for i in range(2)], axis=1
        )
        spectrum = dot(forth, twice(field, 0))
        weights = (first if b == 0 else kernel_ref[b], kernel_ref[b + 1])
        spectrum = jnp.concatenate(
            [(spectrum[:, i * n : (i + 1) * n] * weights[i]).astype(BF) for i in range(2)], axis=1
        )
        mixed = dot(back, twice(spectrum, 0)).astype(BF)
        for p, out in enumerate(outs):
            for i in range(2):
                out[b + i] = mixed[p * planes : (p + 1) * planes, i * n : (i + 1) * n]


def middle(pieces, kernel, extra, forth, back):
    rows, planes, n = pieces[0].shape
    slab = kernel.shape[0]
    piece = pl.BlockSpec((slab, planes, n), lambda i: (i, 0, 0))
    return pl.pallas_call(
        middle_body,
        grid=(rows // slab,),
        in_specs=[piece] * NX
        + [
            pl.BlockSpec(kernel.shape, lambda i: (0, 0, 0)),
            pl.BlockSpec(extra.shape, lambda i: (0, 0, 0)),
            pl.BlockSpec(forth.shape, lambda i: (0, 0)),
            pl.BlockSpec(back.shape, lambda i: (0, 0)),
        ],
        out_specs=[piece] * NX,
        out_shape=[jax.ShapeDtypeStruct((rows, planes, n), BF)] * NX,
        compiler_params=pltpu.CompilerParams(vmem_limit_bytes=VMEM),
        cost_estimate=pl.CostEstimate(flops=0, bytes_accessed=8 << 20, transcendentals=0),
        name="middle",
    )(*pieces, kernel, extra, forth, back)


def inverse_body(p0, p1, p2, p3, occ0, occ1, resp0, resp1, right_ref, left_ref, *rest):
    accumulators, (to0, to1, tr0, tr1, half_ref) = rest[:-5], rest[-5:]
    ins = (p0, p1, p2, p3)
    rows, slab, n = p0.shape
    part_rows = rows * slab

    def part(occ_ref, resp_ref, occ_out, resp_out, occ_in, resp_in):
        right, left = right_ref[...], left_ref[...]
        for p, piece in enumerate(ins):
            field = piece[...].reshape(part_rows, n)
            half_ref[pl.ds(p * part_rows, part_rows), :] = dot(twice(field, 1), right)
        for x in range(0, slab, 2):
            pair = jnp.concatenate(
                [half_ref[pl.ds(x + i, n, stride=slab), :].astype(BF) for i in range(2)], axis=1
            )
            both = dot(left, twice(pair, 0))
            for i in range(2):
                potential = both[:, i * n : (i + 1) * n]
                to_occ = potential * resp_ref[0, x + i].astype(F32)
                to_resp = potential * occ_ref[0, x + i].astype(F32)
                occ_out[0, x + i] = to_occ if occ_in is None else occ_in[0, x + i] + to_occ
                resp_out[0, x + i] = to_resp if resp_in is None else resp_in[0, x + i] + to_resp

    given = [None if a is None else a for a in accumulators]

    @pl.when(pl.program_id(0) == 0)
    def _():
        part(occ0, resp0, to0, tr0, given[0], given[2])

    @pl.when(pl.program_id(0) == 1)
    def _():
        part(occ1, resp1, to1, tr1, given[1], given[3])


def inverse(pieces, occ, resp, right, left, occ_sums, resp_sums):
    rows, planes, n = pieces[0].shape
    slab = planes // 2
    whole = pl.BlockSpec((1, slab, n, n), lambda i: (0, 0, 0, 0))
    sums = [*(occ_sums or (None, None)), *(resp_sums or (None, None))]
    present = [s for s in sums if s is not None]

    def body(*refs):
        refs = list(refs)
        head, tail = refs[:10], refs[10:]
        given = [None if s is None else tail.pop(0) for s in sums]
        inverse_body(*head, *given, *tail)

    return pl.pallas_call(
        body,
        grid=(2,),
        in_specs=[pl.BlockSpec((rows, slab, n), lambda i: (0, i, 0))] * NX
        + [whole] * 4
        + [pl.BlockSpec(right.shape, lambda i: (0, 0)), pl.BlockSpec(left.shape, lambda i: (0, 0))]
        + [whole] * len(present),
        out_specs=[whole] * 4,
        out_shape=[jax.ShapeDtypeStruct((1, slab, n, n), F32)] * 4,
        scratch_shapes=[pltpu.VMEM((slab * n, n), F32)],
        compiler_params=pltpu.CompilerParams(vmem_limit_bytes=VMEM),
        cost_estimate=pl.CostEstimate(flops=0, bytes_accessed=14 << 20, transcendentals=0),
        name="inverse",
    )(*pieces, *occ, *resp, right, left, *present)


def shards(occ_orbitals, occ_mask, resp_orbitals, kernel_index, kernel_table):
    n = occ_orbitals.shape[-1]
    slab = occ_orbitals.shape[1]
    responses = resp_orbitals.shape[0]
    band, grid = lax.axis_index("band"), lax.axis_index("grid")
    core, x, half = band % 2, grid % NX, grid // NX
    counter = jnp.arange(n, dtype=jnp.int32)

    own = jnp.arange(slab, dtype=jnp.int32)[None, :] + slab * (
        half * NX + (x + jnp.arange(NX, dtype=jnp.int32)) % NX
    )[:, None]
    mirrored = (n - own) % n
    mirrored = jnp.where(mirrored == own, (own + n // 2) % n, mirrored)
    frequencies = jnp.concatenate([own, mirrored], axis=1).reshape(-1)
    source = (x - jnp.arange(NX, dtype=jnp.int32)) % NX
    which = jnp.stack([core, 1 - core])
    planes = (
        which[None, :, None] * (NX * slab)
        + source[:, None, None] * slab
        + jnp.arange(slab, dtype=jnp.int32)[None, None, :]
    ).reshape(-1)
    straight = cas(counter, counter, n)
    right = halves(straight, 0)
    right_scaled = halves(straight * (1.0 / float(n**3)), 0)
    left = halves(cas(frequencies, counter, n), 1)
    left_back = halves(cas(counter, frequencies, n), 1)
    forth = halves(cas(counter, planes, n), 1)
    back = halves(cas(planes, counter, n), 1)

    is_low = core == 0

    def pick(low, high):
        return jnp.where(is_low, low, high)

    def after(blocks, *others):
        return lax.optimization_barrier((blocks, others))[0]

    def give_back(block):
        return send(send(block, to_half, back=True), to_place, back=True)

    occupied = occ_orbitals * occ_mask.astype(BF)[:, None, None, None]
    near, far = resp_orbitals[:2], resp_orbitals[2:]
    occ = [None] * STEPS
    occ[0] = send(send(occupied, to_place), to_half)
    near = send(send(near, to_place), to_half)
    near_pair = (pick(near[:1], near[1:]), send(pick(near[1:], near[:1]), to_twin))
    occ_pair = [None] * STEPS
    occ_pair[0] = (occ[0], send(occ[0], to_twin))
    occ[1] = send(after(occ[0], near), to_next)

    edge = send(after(kernel_index[:, 0, :], near), to_mirror)
    edge = jnp.where(x == 0, edge, kernel_index[:, 0, :])
    kernel, extra = lookup(kernel_index, edge, kernel_table)

    def spread(pieces, sign, *others):
        sent = after(tuple(pieces[1:]), *others)
        return [pieces[0]] + [send(p, along_x(sign * s)) for s, p in zip(range(1, NX), sent)]

    def transform(occ_two, resp_two):
        return list(forward(occ_two, resp_two, right, left))

    def weigh(pieces):
        return list(middle(pieces, kernel, extra, forth, back))

    def contract(pieces, occ_two, resp_two, occ_from, resp_from):
        o0, o1, r0, r1 = inverse(pieces, occ_two, resp_two, right_scaled, left_back, occ_from, resp_from)
        return (o0, o1), (r0, r1)

    f0 = spread(transform(occ_pair[0], near_pair), 1)
    occ_pair[1] = (occ[1], send(occ[1], to_twin))
    occ[2] = send(after(occ[0], occ[1]), to_second)
    placed = send(after(far, occ[1]), to_place)
    f1 = spread(transform(occ_pair[1], near_pair), 1)
    b0 = spread(weigh(f0), -1)
    occ_pair[2] = (occ[2], send(occ[2], to_twin))
    occ[3] = send(after(occ[2], f0[1]), to_next)
    f2 = spread(transform(occ_pair[2], near_pair), 1, *f0[1:])
    b1 = spread(weigh(f1), -1)
    sums0, near_sums = contract(b0, occ_pair[0], near_pair, None, None)
    occ_pair[3] = (occ[3], send(occ[3], to_twin))
    far = send(after(placed, occ[3]), to_half)
    f3 = spread(transform(occ_pair[3], near_pair), 1, *b0[1:])
    b2 = spread(weigh(f2), -1, *near_sums)
    sums1, near_sums = contract(b1, occ_pair[1], near_pair, None, near_sums)
    far_pair = (far, send(far, to_twin))
    mixed_pair = [tuple(pick(occ_pair[s][i], occ_pair[s + 1][i]) for i in range(2)) for s in (0, 2)]
    f4 = spread(transform(mixed_pair[1], far_pair), 1, *b1[1:])
    b3 = spread(weigh(f3), -1, *near_sums)
    sums2, near_sums = contract(b2, occ_pair[2], near_pair, None, near_sums)
    f5 = spread(transform(mixed_pair[0], far_pair), 1, *b2[1:])
    b4 = spread(weigh(f4), -1, *near_sums)
    sums3, near_sums = contract(b3, occ_pair[3], near_pair, None, near_sums)
    kept, got = near_sums[0].astype(BF), send(near_sums[1].astype(BF), to_twin)
    near_out = send(jnp.concatenate([pick(kept, got), pick(got, kept)], axis=0), to_half, back=True)
    b5 = spread(weigh(f5), -1, got)
    far_steps, far_sums = contract(b4, mixed_pair[1], far_pair, None, None)

    def merged(low, high, extra_sums):
        zero = jnp.zeros_like(extra_sums[0])
        own = [low[0] + pick(extra_sums[0], zero), high[0] + pick(zero, extra_sums[0])]
        given = [low[1] + pick(extra_sums[1], zero), high[1] + pick(zero, extra_sums[1])]
        got = send(jnp.concatenate(given, axis=0).astype(BF), to_twin).astype(F32)
        return own[0] + got[:1], own[1] + got[1:]

    step2, step3 = merged(sums2, sums3, far_steps)
    step3 = step3.astype(BF)
    total = send(step3, to_next, back=True).astype(F32) + step2
    b5 = after(b5, near_out, step3)
    last, far_sums = contract(b5, mixed_pair[0], far_pair, None, far_sums)
    near_out = send(near_out, to_place, back=True)
    total = send(total.astype(BF), to_second, back=True).astype(F32)
    step0, step1 = merged(sums0, sums1, last)
    total = total + step0 + send(step1.astype(BF), to_next, back=True).astype(F32)
    far_out = (far_sums[0] + send(far_sums[1].astype(BF), to_twin).astype(F32)).astype(BF)
    far_out = give_back(far_out)
    return give_back(total.astype(BF)), jnp.concatenate([near_out, far_out], axis=0)


def solution(mesh):
    in_specs = (
        P("band", "grid", None, None),
        P("band"),
        P("band", "grid", None, None),
        P(None, "grid", None),
        P(),
    )
    out_specs = (P("band", "grid", None, None), P("band", "grid", None, None))
    return jax.shard_map(shards, mesh=mesh, in_specs=in_specs, out_specs=out_specs, check_vma=False)
```

```python
import math

import jax
import jax.numpy as jnp
from jax import lax
from jax.experimental import pallas as pl
from jax.experimental.pallas import tpu as pltpu
from jax.sharding import PartitionSpec as P

BF, F32 = jnp.bfloat16, jnp.float32
STEPS = 4
AXES = ("band", "grid")
NY, NZ, NX = 4, 4, 4
VMEM = 40 << 20


def flat(y, zl, c, h, x):
    return (y * NZ * 2 + zl * 2 + c) * (2 * NX) + h * NX + x


def route(move):
    return [
        (flat(y, zl, c, h, x), flat(*move(y, zl, c, h, x)))
        for y in range(NY)
        for zl in range(NZ)
        for c in range(2)
        for h in range(2)
        for x in range(NX)
    ]


def place(y, c):
    return NY - 1 - y if c else y


def to_place(y, zl, c, h, x):
    return place(y, c), zl, c, h, x


def to_half(y, zl, c, h, x):
    return y, zl, h, c ^ (y // 2), x


def to_next(y, zl, c, h, x):
    core = (y // 2) ^ h
    q = (place(y, core) * NZ * 2 + zl * 2 + core + 1) % (NY * NZ * 2)
    y, zl, core = q // (2 * NZ), q // 2 % NZ, q % 2
    return place(y, core), zl, c, y // 2, x


def to_second(*at):
    return to_next(*to_next(*at))


def to_twin(y, zl, c, h, x):
    return y, zl, 1 - c, h, x


def to_mirror(y, zl, c, h, x):
    return y, zl, c, 1 - h, x


def along_x(distance):
    return lambda y, zl, c, h, x: (y, zl, c, h, (x + distance) % NX)


def send(block, move, back=False):
    pairs = route(move)
    return lax.ppermute(block, AXES, [(b, a) for a, b in pairs] if back else pairs)


def cas(rows, columns, length):
    product = (rows[:, None] * columns[None, :]) % length
    angles = (2.0 * math.pi / length) * product.astype(F32)
    return jnp.cos(angles) + jnp.sin(angles)


def halves(table, axis):
    high = lax.reduce_precision(table, 8, 7)
    return jnp.concatenate([high.astype(BF), (table - high).astype(BF)], axis=axis)


def dot(a, b):
    return jnp.dot(a, b, preferred_element_type=F32)


def twice(block, axis):
    return jnp.concatenate([block, block], axis=axis)


def lookup_body(index_ref, mirror_ref, table_ref, out_ref, extra_ref):
    n, slab, _ = extra_ref.shape[1], out_ref.shape[0], None
    table = jnp.broadcast_to(table_ref[...], (n, n))
    for b in range(slab):
        entry = index_ref[pl.ds(b, n, stride=slab), :]
        out_ref[b] = jnp.take_along_axis(table, entry, axis=1, mode="promise_in_bounds")
    extra_ref[0] = jnp.take_along_axis(table, mirror_ref[...], axis=1, mode="promise_in_bounds")


def lookup(index, mirror, table):
    n, slab, _ = index.shape
    row = jnp.zeros((1, n), F32).at[0, : table.shape[0]].set(table)
    return pl.pallas_call(
        lookup_body,
        out_shape=[jax.ShapeDtypeStruct((slab, n, n), F32), jax.ShapeDtypeStruct((1, n, n), F32)],
        compiler_params=pltpu.CompilerParams(vmem_limit_bytes=VMEM),
        cost_estimate=pl.CostEstimate(flops=0, bytes_accessed=8 << 20, transcendentals=0),
        name="lookup",
    )(index.reshape(n * slab, n), mirror, row)


def forward_body(occ0, occ1, resp0, resp1, right_ref, left_ref, *rest):
    outs, half_ref = rest[:-1], rest[-1]
    slab, n = occ0.shape[1], occ0.shape[3]
    per = n // len(outs)

    def part(occ_ref, resp_ref):
        density = (occ_ref[0] * resp_ref[0]).reshape(slab * n, n)
        along = dot(twice(density, 1), right_ref[...]).astype(BF)
        left = left_ref[...]
        for x in range(0, slab, 2):
            pair = jnp.concatenate([along[(x + i) * n : (x + i + 1) * n] for i in range(2)], axis=1)
            both = dot(left, twice(pair, 0))
            for i in range(2):
                half_ref[pl.ds((x + i) * n, n), :] = both[:, i * n : (i + 1) * n]
        for b in range(n):
            outs[b // per][b % per] = half_ref[pl.ds(b, slab, stride=n), :].astype(BF)

    @pl.when(pl.program_id(0) == 0)
    def _():
        part(occ0, resp0)

    @pl.when(pl.program_id(0) == 1)
    def _():
        part(occ1, resp1)


def forward(occ, resp, right, left):
    _, slab, n, _ = occ[0].shape
    per = n // NX
    whole = pl.BlockSpec((1, slab, n, n), lambda i: (0, 0, 0, 0))
    return pl.pallas_call(
        forward_body,
        grid=(2,),
        in_specs=[whole] * 4
        + [pl.BlockSpec(right.shape, lambda i: (0, 0)), pl.BlockSpec(left.shape, lambda i: (0, 0))],
        out_specs=[pl.BlockSpec((per, slab, n), lambda i: (0, i, 0))] * NX,
        out_shape=[jax.ShapeDtypeStruct((per, 2 * slab, n), BF)] * NX,
        scratch_shapes=[pltpu.VMEM((slab * n, n), F32)],
        compiler_params=pltpu.CompilerParams(vmem_limit_bytes=VMEM),
        cost_estimate=pl.CostEstimate(flops=0, bytes_accessed=12 << 20, transcendentals=0),
        name="forward",
    )(*occ, *resp, right, left)


def middle_body(p0, p1, p2, p3, kernel_ref, extra_ref, forth_ref, back_ref, *outs):
    ins = (p0, p1, p2, p3)
    rows, planes, n = p0.shape
    forth, back = forth_ref[...], back_ref[...]
    first = jnp.where(pl.program_id(0) == 0, kernel_ref[0], extra_ref[0])
    for b in range(0, rows, 2):
        field = jnp.concatenate(
            [jnp.concatenate([r[b + i] for r in ins], axis=0) for i in range(2)], axis=1
        )
        spectrum = dot(forth, twice(field, 0))
        weights = (first if b == 0 else kernel_ref[b], kernel_ref[b + 1])
        spectrum = jnp.concatenate(
            [(spectrum[:, i * n : (i + 1) * n] * weights[i]).astype(BF) for i in range(2)], axis=1
        )
        mixed = dot(back, twice(spectrum, 0)).astype(BF)
        for p, out in enumerate(outs):
            for i in range(2):
                out[b + i] = mixed[p * planes : (p + 1) * planes, i * n : (i + 1) * n]


def middle(pieces, kernel, extra, forth, back):
    rows, planes, n = pieces[0].shape
    slab = kernel.shape[0]
    piece = pl.BlockSpec((slab, planes, n), lambda i: (i, 0, 0))
    return pl.pallas_call(
        middle_body,
        grid=(rows // slab,),
        in_specs=[piece] * NX
        + [
            pl.BlockSpec(kernel.shape, lambda i: (0, 0, 0)),
            pl.BlockSpec(extra.shape, lambda i: (0, 0, 0)),
            pl.BlockSpec(forth.shape, lambda i: (0, 0)),
            pl.BlockSpec(back.shape, lambda i: (0, 0)),
        ],
        out_specs=[piece] * NX,
        out_shape=[jax.ShapeDtypeStruct((rows, planes, n), BF)] * NX,
        compiler_params=pltpu.CompilerParams(vmem_limit_bytes=VMEM),
        cost_estimate=pl.CostEstimate(flops=0, bytes_accessed=8 << 20, transcendentals=0),
        name="middle",
    )(*pieces, kernel, extra, forth, back)


def inverse_body(p0, p1, p2, p3, occ0, occ1, resp0, resp1, right_ref, left_ref, *rest):
    accumulators, (to0, to1, tr0, tr1, half_ref) = rest[:-5], rest[-5:]
    ins = (p0, p1, p2, p3)
    rows, slab, n = p0.shape
    part_rows = rows * slab

    def part(occ_ref, resp_ref, occ_out, resp_out, occ_in, resp_in):
        right, left = right_ref[...], left_ref[...]
        for p, piece in enumerate(ins):
            field = piece[...].reshape(part_rows, n)
            half_ref[pl.ds(p * part_rows, part_rows), :] = dot(twice(field, 1), right)
        for x in range(0, slab, 2):
            pair = jnp.concatenate(
                [half_ref[pl.ds(x + i, n, stride=slab), :].astype(BF) for i in range(2)], axis=1
            )
            both = dot(left, twice(pair, 0))
            for i in range(2):
                potential = both[:, i * n : (i + 1) * n]
                to_occ = potential * resp_ref[0, x + i].astype(F32)
                to_resp = potential * occ_ref[0, x + i].astype(F32)
                occ_out[0, x + i] = to_occ if occ_in is None else occ_in[0, x + i] + to_occ
                resp_out[0, x + i] = to_resp if resp_in is None else resp_in[0, x + i] + to_resp

    given = [None if a is None else a for a in accumulators]

    @pl.when(pl.program_id(0) == 0)
    def _():
        part(occ0, resp0, to0, tr0, given[0], given[2])

    @pl.when(pl.program_id(0) == 1)
    def _():
        part(occ1, resp1, to1, tr1, given[1], given[3])


def inverse(pieces, occ, resp, right, left, occ_sums, resp_sums):
    rows, planes, n = pieces[0].shape
    slab = planes // 2
    whole = pl.BlockSpec((1, slab, n, n), lambda i: (0, 0, 0, 0))
    sums = [*(occ_sums or (None, None)), *(resp_sums or (None, None))]
    present = [s for s in sums if s is not None]

    def body(*refs):
        refs = list(refs)
        head, tail = refs[:10], refs[10:]
        given = [None if s is None else tail.pop(0) for s in sums]
        inverse_body(*head, *given, *tail)

    return pl.pallas_call(
        body,
        grid=(2,),
        in_specs=[pl.BlockSpec((rows, slab, n), lambda i: (0, i, 0))] * NX
        + [whole] * 4
        + [pl.BlockSpec(right.shape, lambda i: (0, 0)), pl.BlockSpec(left.shape, lambda i: (0, 0))]
        + [whole] * len(present),
        out_specs=[whole] * 4,
        out_shape=[jax.ShapeDtypeStruct((1, slab, n, n), F32)] * 4,
        scratch_shapes=[pltpu.VMEM((slab * n, n), F32)],
        compiler_params=pltpu.CompilerParams(vmem_limit_bytes=VMEM),
        cost_estimate=pl.CostEstimate(flops=0, bytes_accessed=14 << 20, transcendentals=0),
        name="inverse",
    )(*pieces, *occ, *resp, right, left, *present)


def shards(occ_orbitals, occ_mask, resp_orbitals, kernel_index, kernel_table):
    n = occ_orbitals.shape[-1]
    slab = occ_orbitals.shape[1]
    responses = resp_orbitals.shape[0]
    band, grid = lax.axis_index("band"), lax.axis_index("grid")
    core, x, half = band % 2, grid % NX, grid // NX
    counter = jnp.arange(n, dtype=jnp.int32)

    own = jnp.arange(slab, dtype=jnp.int32)[None, :] + slab * (
        half * NX + (x + jnp.arange(NX, dtype=jnp.int32)) % NX
    )[:, None]
    mirrored = (n - own) % n
    mirrored = jnp.where(mirrored == own, (own + n // 2) % n, mirrored)
    frequencies = jnp.concatenate([own, mirrored], axis=1).reshape(-1)
    source = (x - jnp.arange(NX, dtype=jnp.int32)) % NX
    which = jnp.stack([core, 1 - core])
    planes = (
        which[None, :, None] * (NX * slab)
        + source[:, None, None] * slab
        + jnp.arange(slab, dtype=jnp.int32)[None, None, :]
    ).reshape(-1)
    straight = cas(counter, counter, n)
    right = halves(straight, 0)
    right_scaled = halves(straight * (1.0 / float(n**3)), 0)
    left = halves(cas(frequencies, counter, n), 1)
    left_back = halves(cas(counter, frequencies, n), 1)
    forth = halves(cas(counter, planes, n), 1)
    back = halves(cas(planes, counter, n), 1)

    is_low = core == 0

    def pick(low, high):
        return jnp.where(is_low, low, high)

    def after(blocks, *others):
        return lax.optimization_barrier((blocks, others))[0]

    def give_back(block):
        return send(send(block, to_half, back=True), to_place, back=True)

    occupied = occ_orbitals * occ_mask.astype(BF)[:, None, None, None]
    near, far = resp_orbitals[:2], resp_orbitals[2:]
    occ, occ_pair = [None] * STEPS, [None] * STEPS
    occ[0] = send(occupied, to_place)
    near = send(near, to_place)
    edge = send(kernel_index[:, 0, :], to_mirror)
    edge = jnp.where(x == 0, edge, kernel_index[:, 0, :])
    kernel, extra = lookup(kernel_index, edge, kernel_table)
    occ[0] = send(after(occ[0], edge), to_half)
    near = send(near, to_half)
    near_pair = (pick(near[:1], near[1:]), send(pick(near[1:], near[:1]), to_twin))
    occ_pair[0] = (occ[0], send(occ[0], to_twin))
    occ[1] = send(after(occ[0], near), to_next)

    def spread(pieces, sign, *others):
        sent = after(tuple(pieces[1:]), *others)
        return [pieces[0]] + [send(p, along_x(sign * s)) for s, p in zip(range(1, NX), sent)]

    def transform(occ_two, resp_two):
        return list(forward(occ_two, resp_two, right, left))

    def weigh(pieces):
        return list(middle(pieces, kernel, extra, forth, back))

    def contract(pieces, occ_two, resp_two, occ_from, resp_from):
        o0, o1, r0, r1 = inverse(pieces, occ_two, resp_two, right_scaled, left_back, occ_from, resp_from)
        return (o0, o1), (r0, r1)

    t0 = transform(after(occ_pair[0], kernel), near_pair)
    f0 = spread(t0, 1)
    occ[1] = after(occ[1], *t0)
    occ_pair[1] = (occ[1], send(occ[1], to_twin))
    occ[2] = send(after(occ[0], occ[1]), to_second)
    placed = send(after(far, occ[1]), to_place)
    f1 = spread(transform(occ_pair[1], near_pair), 1)
    b0 = spread(weigh(f0), -1)
    occ_pair[2] = (occ[2], send(occ[2], to_twin))
    occ[3] = send(after(occ[2], f0[1]), to_next)
    f2 = spread(transform(occ_pair[2], near_pair), 1, *f0[1:])
    b1 = spread(weigh(f1), -1)
    sums0, near_sums = contract(b0, occ_pair[0], near_pair, None, None)
    occ_pair[3] = (occ[3], send(occ[3], to_twin))
    far = send(after(placed, occ[3]), to_half)
    f3 = spread(transform(occ_pair[3], near_pair), 1, *b0[1:])
    b2 = spread(weigh(f2), -1, *near_sums)
    sums1, near_sums = contract(b1, occ_pair[1], near_pair, None, near_sums)
    far_pair = (far, send(far, to_twin))
    mixed_pair = [tuple(pick(occ_pair[s][i], occ_pair[s + 1][i]) for i in range(2)) for s in (0, 2)]
    t4 = transform(mixed_pair[1], far_pair)
    f4 = spread(t4, 1, *b1[1:])
    b3 = spread(weigh(f3), -1, *near_sums)
    sums2, near_sums = contract(after(b2, *t4), occ_pair[2], near_pair, None, near_sums)
    t5 = transform(mixed_pair[0], far_pair)
    f5 = spread(t5, 1, *b2[1:])
    b4 = spread(weigh(f4), -1, *near_sums)
    sums3, near_sums = contract(after(b3, *t5), occ_pair[3], near_pair, None, near_sums)
    kept, got = near_sums[0].astype(BF), send(near_sums[1].astype(BF), to_twin)
    near_out = send(jnp.concatenate([pick(kept, got), pick(got, kept)], axis=0), to_half, back=True)
    b5 = spread(weigh(f5), -1, got)
    far_steps, far_sums = contract(b4, mixed_pair[1], far_pair, None, None)

    def merged(low, high, extra_sums):
        zero = jnp.zeros_like(extra_sums[0])
        own = [low[0] + pick(extra_sums[0], zero), high[0] + pick(zero, extra_sums[0])]
        given = [low[1] + pick(extra_sums[1], zero), high[1] + pick(zero, extra_sums[1])]
        got = send(jnp.concatenate(given, axis=0).astype(BF), to_twin).astype(F32)
        return own[0] + got[:1], own[1] + got[1:]

    step2, step3 = merged(sums2, sums3, far_steps)
    step3 = step3.astype(BF)
    total = send(step3, to_next, back=True)
    b5 = after(b5, near_out, step3)
    last, far_sums = contract(b5, mixed_pair[0], far_pair, None, far_sums)
    near_out = send(near_out, to_place, back=True)
    step0, step1 = merged(sums0, sums1, last)
    step1 = step1.astype(BF)
    far_out = (far_sums[0] + send(far_sums[1].astype(BF), to_twin).astype(F32)).astype(BF)
    total = (after(total, step1, far_out).astype(F32) + step2).astype(BF)
    total = send(total, to_second, back=True).astype(F32)
    total = total + step0 + send(after(step1, far_out), to_next, back=True).astype(F32)
    far_out = give_back(far_out)
    return give_back(total.astype(BF)), jnp.concatenate([near_out, far_out], axis=0)


def solution(mesh):
    in_specs = (
        P("band", "grid", None, None),
        P("band"),
        P("band", "grid", None, None),
        P(None, "grid", None),
        P(),
    )
    out_specs = (P("band", "grid", None, None), P("band", "grid", None, None))
    return jax.shard_map(shards, mesh=mesh, in_specs=in_specs, out_specs=out_specs, check_vma=False)
```

```python
import math

import jax
import jax.numpy as jnp
from jax import lax
from jax.experimental import pallas as pl
from jax.experimental.pallas import tpu as pltpu
from jax.sharding import PartitionSpec as P

BF, F32 = jnp.bfloat16, jnp.float32
STEPS = 4
VMEM = 40 << 20


def shifted(block, distance):
    devices = lax.axis_size("band")
    return lax.ppermute(block, "band", [((i - distance) % devices, i) for i in range(devices)])


def cas(length):
    counter = jnp.arange(length, dtype=jnp.int32)
    product = (counter[:, None] * counter[None, :]) % length
    angles = (2.0 * math.pi / length) * product.astype(F32)
    return jnp.cos(angles) + jnp.sin(angles)


def halves(table, axis):
    high = lax.reduce_precision(table, 8, 7)
    return jnp.concatenate([high.astype(BF), (table - high).astype(BF)], axis=axis)


def dot(a, b):
    return jnp.dot(a, b, preferred_element_type=F32)


def twice(block, axis):
    return jnp.concatenate([block, block], axis=axis)


def lookup_body(index_ref, table_ref, out_ref):
    slab, n, _ = out_ref.shape
    table = jnp.broadcast_to(table_ref[...], (n, n))
    for b in range(slab):
        entry = index_ref[pl.ds(b, n, stride=slab), :]
        out_ref[b] = jnp.take_along_axis(table, entry, axis=1, mode="promise_in_bounds")


def lookup(index, table):
    n, slab, _ = index.shape
    row = jnp.zeros((1, n), F32).at[0, : table.shape[0]].set(table)
    return pl.pallas_call(
        lookup_body,
        out_shape=jax.ShapeDtypeStruct((slab, n, n), F32),
        compiler_params=pltpu.CompilerParams(vmem_limit_bytes=VMEM),
        cost_estimate=cost(1),
        name="lookup",
    )(index.reshape(n * slab, n), row)


def cost(microseconds):
    return pl.CostEstimate(flops=0, bytes_accessed=microseconds * 3_600_000, transcendentals=0)


def fixed(shape):
    return pl.BlockSpec(shape, lambda i: (0,) * len(shape))


def distinct(items):
    return sorted(set(items))


def forward(chunk, occ, resp, right, left):
    _, slab, n, _ = occ[0].shape
    peers = n // slab
    steps, members = distinct(s for s, _ in chunk), distinct(j for _, j in chunk)

    def body(*refs):
        occ_refs = dict(zip(steps, refs))
        resp_refs = dict(zip(members, refs[len(steps) :]))
        right_ref, left_ref, out, half_ref = refs[len(steps) + len(members) :]

        def part(occ_ref, resp_ref):
            density = (occ_ref[0] * resp_ref[0]).reshape(slab * n, n)
            along = dot(twice(density, 1), right_ref[...]).astype(BF)
            left = left_ref[...]
            for x in range(0, slab, 2):
                pair = jnp.concatenate([along[(x + i) * n : (x + i + 1) * n] for i in range(2)], axis=1)
                both = dot(left, twice(pair, 0))
                for i in range(2):
                    half_ref[pl.ds((x + i) * n, n), :] = both[:, i * n : (i + 1) * n]
            for b in range(n):
                out[b // slab, 0, b % slab] = half_ref[pl.ds(b, slab, stride=n), :].astype(BF)

        for p, (s, j) in enumerate(chunk):
            pl.when(pl.program_id(0) == p)(lambda s=s, j=j: part(occ_refs[s], resp_refs[j]))

    return pl.pallas_call(
        body,
        grid=(len(chunk),),
        in_specs=[fixed(occ[0].shape)] * (len(steps) + len(members)) + [fixed(right.shape), fixed(left.shape)],
        out_specs=pl.BlockSpec((peers, 1, slab, slab, n), lambda i: (0, i, 0, 0, 0)),
        out_shape=jax.ShapeDtypeStruct((peers, len(chunk), slab, slab, n), BF),
        scratch_shapes=[pltpu.VMEM((slab * n, n), F32)],
        compiler_params=pltpu.CompilerParams(vmem_limit_bytes=VMEM),
        cost_estimate=cost(2 * len(chunk)),
        name="forward",
    )(*[occ[s] for s in steps], *[resp[j] for j in members], right, left)


def middle_body(field_ref, kernel_ref, table_ref, out):
    peers, _, rows, slab, n = field_ref.shape
    table = table_ref[...]
    for b in range(0, rows, 2):
        field = jnp.concatenate(
            [jnp.concatenate([field_ref[p, 0, b + i] for p in range(peers)], axis=0) for i in range(2)], axis=1
        )
        spectrum = dot(table, twice(field, 0))
        spectrum = jnp.concatenate(
            [(spectrum[:, i * n : (i + 1) * n] * kernel_ref[b + i]).astype(BF) for i in range(2)], axis=1
        )
        mixed = dot(table, twice(spectrum, 0)).astype(BF)
        for p in range(peers):
            for i in range(2):
                out[p, 0, b + i] = mixed[p * slab : (p + 1) * slab, i * n : (i + 1) * n]


def middle(field, kernel, table):
    peers, count, rows, slab, n = field.shape
    piece = pl.BlockSpec((peers, 1, rows, slab, n), lambda i: (0, i, 0, 0, 0))
    return pl.pallas_call(
        middle_body,
        grid=(count,),
        in_specs=[piece, fixed(kernel.shape), fixed(table.shape)],
        out_specs=piece,
        out_shape=jax.ShapeDtypeStruct(field.shape, BF),
        compiler_params=pltpu.CompilerParams(vmem_limit_bytes=VMEM),
        cost_estimate=cost(count),
        name="middle",
    )(field, kernel, table)


def inverse(chunk, field, occ, resp, right, left, occ_sums, resp_sums):
    peers, _, rows, slab, n = field.shape
    steps, members = distinct(s for s, _ in chunk), distinct(j for _, j in chunk)
    old_steps = [s for s in steps if occ_sums[s] is not None]
    old_members = [j for j in members if resp_sums[j] is not None]

    def body(field_ref, right_ref, left_ref, *refs):
        refs, half_ref = list(refs[:-1]), refs[-1]

        def take(keys):
            return {k: refs.pop(0) for k in keys}

        occ_refs, resp_refs = take(steps), take(members)
        occ_in, resp_in = take(old_steps), take(old_members)
        occ_out, resp_out = take(steps), take(members)

        def part(occ_ref, resp_ref, occ_from, occ_to, resp_from, resp_to):
            right, left = right_ref[...], left_ref[...]
            flat_field = field_ref[:, 0].reshape(peers * rows * slab, n)
            half_ref[...] = dot(twice(flat_field, 1), right)
            for x in range(0, slab, 2):
                pair = jnp.concatenate(
                    [half_ref[pl.ds(x + i, n, stride=slab), :].astype(BF) for i in range(2)], axis=1
                )
                both = dot(left, twice(pair, 0))
                for i in range(2):
                    potential = both[:, i * n : (i + 1) * n]
                    to_occ = potential * resp_ref[0, x + i].astype(F32)
                    to_resp = potential * occ_ref[0, x + i].astype(F32)
                    occ_to[0, x + i] = to_occ if occ_from is None else occ_from[0, x + i] + to_occ
                    resp_to[0, x + i] = to_resp if resp_from is None else resp_from[0, x + i] + to_resp

        for p, (s, j) in enumerate(chunk):
            occ_from = occ_out[s] if s in [k for k, _ in chunk[:p]] else occ_in.get(s)
            resp_from = resp_out[j] if j in [k for _, k in chunk[:p]] else resp_in.get(j)

            def run(s=s, j=j, occ_from=occ_from, resp_from=resp_from):
                part(occ_refs[s], resp_refs[j], occ_from, occ_out[s], resp_from, resp_out[j])

            pl.when(pl.program_id(0) == p)(run)

    whole = fixed(occ[0].shape)
    ends = len(steps) + len(members)
    out = pl.pallas_call(
        body,
        grid=(len(chunk),),
        in_specs=[pl.BlockSpec((peers, 1, rows, slab, n), lambda i: (0, i, 0, 0, 0)), fixed(right.shape), fixed(left.shape)]
        + [whole] * (ends + len(old_steps) + len(old_members)),
        out_specs=[whole] * ends,
        out_shape=[jax.ShapeDtypeStruct(occ[0].shape, F32)] * ends,
        scratch_shapes=[pltpu.VMEM((slab * n, n), F32)],
        compiler_params=pltpu.CompilerParams(vmem_limit_bytes=VMEM),
        cost_estimate=cost(2 * len(chunk)),
        name="inverse",
    )(
        field,
        right,
        left,
        *[occ[s] for s in steps],
        *[resp[j] for j in members],
        *[occ_sums[s] for s in old_steps],
        *[resp_sums[j] for j in old_members],
    )
    for k, s in enumerate(steps):
        occ_sums[s] = out[k]
    for k, j in enumerate(members):
        resp_sums[j] = out[len(steps) + k]


def exchange(field, *others):
    field = after(field, *others)
    return lax.all_to_all(field, "grid", split_axis=0, concat_axis=0, tiled=True)


def after(block, *others):
    return lax.optimization_barrier((block, others))[0]


def shards(occ_orbitals, occ_mask, resp_orbitals, kernel_index, kernel_table):
    n = occ_orbitals.shape[-1]
    responses = resp_orbitals.shape[0]
    straight = cas(n)
    right, left = halves(straight, 0), halves(straight, 1)
    right_scaled = halves(straight * (1.0 / float(n**3)), 0)
    occ = [occ_orbitals * occ_mask.astype(BF)[:, None, None, None]]
    resp = [resp_orbitals[j : j + 1] for j in range(responses)]
    for _ in range(STEPS - 1):
        occ.append(shifted(occ[-1], 1))
    chunks = [[(s, j) for j in range(responses)] for s in range(STEPS)]

    kernel = lookup(kernel_index, kernel_table)
    fields, done = [], []
    for s in range(STEPS):
        ready = done[-2:-1] if s else occ[1:3]
        fields.append(exchange(forward(chunks[s], occ, resp, right, left), *ready))
        done.append(fields[-1])
    occ_sums, resp_sums = [None] * STEPS, [None] * responses
    order, returned = [2, 3, 1, 0], []
    for i, s in enumerate(order):
        ready = done[-2:-1]
        if i > 1:
            last = order[i - 2]
            inverse(chunks[last], fields[last], occ, resp, right_scaled, left, occ_sums, resp_sums)
            returned.append(shifted(occ_sums[last].astype(BF), -last))
            ready = ready + resp_sums
        fields[s] = exchange(middle(fields[s], kernel, left), *ready)
        done.append(fields[s])
    inverse(chunks[1], after(fields[1], returned[0]), occ, resp, right_scaled, left, occ_sums, resp_sums)
    returned.append(shifted(occ_sums[1].astype(BF), -1))
    inverse(chunks[0], after(fields[0], returned[1]), occ, resp, right_scaled, left, occ_sums, resp_sums)
    total = occ_sums[0] + sum(r.astype(F32) for r in returned)
    return total.astype(BF), jnp.concatenate(resp_sums, axis=0).astype(BF)


def solution(mesh):
    in_specs = (
        P("band", "grid", None, None),
        P("band"),
        P("band", "grid", None, None),
        P(None, "grid", None),
        P(),
    )
    out_specs = (P("band", "grid", None, None), P("band", "grid", None, None))
    return jax.shard_map(shards, mesh=mesh, in_specs=in_specs, out_specs=out_specs, check_vma=False)
```

```python
import math

import jax
import jax.numpy as jnp
from jax import lax
from jax.experimental import pallas as pl
from jax.experimental.pallas import tpu as pltpu
from jax.sharding import PartitionSpec as P

BF, F32 = jnp.bfloat16, jnp.float32
STEPS = 4
VMEM = 40 << 20


def shifted(block, distance):
    devices = lax.axis_size("band")
    return lax.ppermute(block, "band", [((i - distance) % devices, i) for i in range(devices)])


def cas(length):
    counter = jnp.arange(length, dtype=jnp.int32)
    product = (counter[:, None] * counter[None, :]) % length
    angles = (2.0 * math.pi / length) * product.astype(F32)
    return jnp.cos(angles) + jnp.sin(angles)


def halves(table, axis):
    high = lax.reduce_precision(table, 8, 7)
    return jnp.concatenate([high.astype(BF), (table - high).astype(BF)], axis=axis)


def dot(a, b):
    return jnp.dot(a, b, preferred_element_type=F32)


def twice(block, axis):
    return jnp.concatenate([block, block], axis=axis)


def lookup_body(index_ref, table_ref, out_ref):
    slab, n, _ = out_ref.shape
    table = jnp.broadcast_to(table_ref[...], (n, n))
    for b in range(slab):
        entry = index_ref[pl.ds(b, n, stride=slab), :]
        out_ref[b] = jnp.take_along_axis(table, entry, axis=1, mode="promise_in_bounds")


def lookup(index, table):
    n, slab, _ = index.shape
    row = jnp.zeros((1, n), F32).at[0, : table.shape[0]].set(table)
    return pl.pallas_call(
        lookup_body,
        out_shape=jax.ShapeDtypeStruct((slab, n, n), F32),
        compiler_params=pltpu.CompilerParams(vmem_limit_bytes=VMEM),
        cost_estimate=cost(1),
        name="lookup",
    )(index.reshape(n * slab, n), row)


def cost(microseconds):
    return pl.CostEstimate(flops=0, bytes_accessed=microseconds * 3_600_000, transcendentals=0)


def fixed(shape):
    return pl.BlockSpec(shape, lambda i: (0,) * len(shape))


def distinct(items):
    return sorted(set(items))


def forward(chunk, occ, resp, right, left):
    _, slab, n, _ = occ[0].shape
    peers = n // slab
    steps, members = distinct(s for s, _ in chunk), distinct(j for _, j in chunk)

    def body(*refs):
        occ_refs = dict(zip(steps, refs))
        resp_refs = dict(zip(members, refs[len(steps) :]))
        right_ref, left_ref, out, half_ref = refs[len(steps) + len(members) :]

        def part(occ_ref, resp_ref):
            density = (occ_ref[0] * resp_ref[0]).reshape(slab * n, n)
            along = dot(twice(density, 1), right_ref[...]).astype(BF)
            left = left_ref[...]
            for x in range(0, slab, 2):
                pair = jnp.concatenate([along[(x + i) * n : (x + i + 1) * n] for i in range(2)], axis=1)
                both = dot(left, twice(pair, 0))
                for i in range(2):
                    half_ref[pl.ds((x + i) * n, n), :] = both[:, i * n : (i + 1) * n]
            for b in range(n):
                out[b // slab, 0, b % slab] = half_ref[pl.ds(b, slab, stride=n), :].astype(BF)

        for p, (s, j) in enumerate(chunk):
            pl.when(pl.program_id(0) == p)(lambda s=s, j=j: part(occ_refs[s], resp_refs[j]))

    return pl.pallas_call(
        body,
        grid=(len(chunk),),
        in_specs=[fixed(occ[0].shape)] * (len(steps) + len(members)) + [fixed(right.shape), fixed(left.shape)],
        out_specs=pl.BlockSpec((peers, 1, slab, slab, n), lambda i: (0, i, 0, 0, 0)),
        out_shape=jax.ShapeDtypeStruct((peers, len(chunk), slab, slab, n), BF),
        scratch_shapes=[pltpu.VMEM((slab * n, n), F32)],
        compiler_params=pltpu.CompilerParams(vmem_limit_bytes=VMEM),
        cost_estimate=cost(2 * len(chunk)),
        name="forward",
    )(*[occ[s] for s in steps], *[resp[j] for j in members], right, left)


def middle_body(field_ref, kernel_ref, table_ref, out):
    peers, _, rows, slab, n = field_ref.shape
    table = table_ref[...]
    for b in range(0, rows, 2):
        field = jnp.concatenate(
            [jnp.concatenate([field_ref[p, 0, b + i] for p in range(peers)], axis=0) for i in range(2)], axis=1
        )
        spectrum = dot(table, twice(field, 0))
        spectrum = jnp.concatenate(
            [(spectrum[:, i * n : (i + 1) * n] * kernel_ref[b + i]).astype(BF) for i in range(2)], axis=1
        )
        mixed = dot(table, twice(spectrum, 0)).astype(BF)
        for p in range(peers):
            for i in range(2):
                out[p, 0, b + i] = mixed[p * slab : (p + 1) * slab, i * n : (i + 1) * n]


def middle(field, kernel, table):
    peers, count, rows, slab, n = field.shape
    piece = pl.BlockSpec((peers, 1, rows, slab, n), lambda i: (0, i, 0, 0, 0))
    return pl.pallas_call(
        middle_body,
        grid=(count,),
        in_specs=[piece, fixed(kernel.shape), fixed(table.shape)],
        out_specs=piece,
        out_shape=jax.ShapeDtypeStruct(field.shape, BF),
        compiler_params=pltpu.CompilerParams(vmem_limit_bytes=VMEM),
        cost_estimate=cost(count),
        name="middle",
    )(field, kernel, table)


def inverse(chunk, field, occ, resp, right, left, occ_sums, resp_sums):
    peers, _, rows, slab, n = field.shape
    steps, members = distinct(s for s, _ in chunk), distinct(j for _, j in chunk)
    old_steps = [s for s in steps if occ_sums[s] is not None]
    old_members = [j for j in members if resp_sums[j] is not None]

    def body(field_ref, right_ref, left_ref, *refs):
        refs, half_ref = list(refs[:-1]), refs[-1]

        def take(keys):
            return {k: refs.pop(0) for k in keys}

        occ_refs, resp_refs = take(steps), take(members)
        occ_in, resp_in = take(old_steps), take(old_members)
        occ_out, resp_out = take(steps), take(members)

        def part(occ_ref, resp_ref, occ_from, occ_to, resp_from, resp_to):
            right, left = right_ref[...], left_ref[...]
            flat_field = field_ref[:, 0].reshape(peers * rows * slab, n)
            half_ref[...] = dot(twice(flat_field, 1), right)
            for x in range(0, slab, 2):
                pair = jnp.concatenate(
                    [half_ref[pl.ds(x + i, n, stride=slab), :].astype(BF) for i in range(2)], axis=1
                )
                both = dot(left, twice(pair, 0))
                for i in range(2):
                    potential = both[:, i * n : (i + 1) * n]
                    to_occ = potential * resp_ref[0, x + i].astype(F32)
                    to_resp = potential * occ_ref[0, x + i].astype(F32)
                    occ_to[0, x + i] = to_occ if occ_from is None else occ_from[0, x + i] + to_occ
                    resp_to[0, x + i] = to_resp if resp_from is None else resp_from[0, x + i] + to_resp

        for p, (s, j) in enumerate(chunk):
            occ_from = occ_out[s] if s in [k for k, _ in chunk[:p]] else occ_in.get(s)
            resp_from = resp_out[j] if j in [k for _, k in chunk[:p]] else resp_in.get(j)

            def run(s=s, j=j, occ_from=occ_from, resp_from=resp_from):
                part(occ_refs[s], resp_refs[j], occ_from, occ_out[s], resp_from, resp_out[j])

            pl.when(pl.program_id(0) == p)(run)

    whole = fixed(occ[0].shape)
    ends = len(steps) + len(members)
    out = pl.pallas_call(
        body,
        grid=(len(chunk),),
        in_specs=[pl.BlockSpec((peers, 1, rows, slab, n), lambda i: (0, i, 0, 0, 0)), fixed(right.shape), fixed(left.shape)]
        + [whole] * (ends + len(old_steps) + len(old_members)),
        out_specs=[whole] * ends,
        out_shape=[jax.ShapeDtypeStruct(occ[0].shape, F32)] * ends,
        scratch_shapes=[pltpu.VMEM((slab * n, n), F32)],
        compiler_params=pltpu.CompilerParams(vmem_limit_bytes=VMEM),
        cost_estimate=cost(2 * len(chunk)),
        name="inverse",
    )(
        field,
        right,
        left,
        *[occ[s] for s in steps],
        *[resp[j] for j in members],
        *[occ_sums[s] for s in old_steps],
        *[resp_sums[j] for j in old_members],
    )
    for k, s in enumerate(steps):
        occ_sums[s] = out[k]
    for k, j in enumerate(members):
        resp_sums[j] = out[len(steps) + k]


def exchange(field, *others):
    field = after(field, *others)
    return lax.all_to_all(field, "grid", split_axis=0, concat_axis=0, tiled=True)


def after(block, *others):
    return lax.optimization_barrier((block, others))[0]


def shards(occ_orbitals, occ_mask, resp_orbitals, kernel_index, kernel_table):
    n = occ_orbitals.shape[-1]
    responses = resp_orbitals.shape[0]
    straight = cas(n)
    right, left = halves(straight, 0), halves(straight, 1)
    right_scaled = halves(straight * (1.0 / float(n**3)), 0)
    occ = [occ_orbitals * occ_mask.astype(BF)[:, None, None, None]]
    resp = [resp_orbitals[j : j + 1] for j in range(responses)]
    for _ in range(STEPS - 1):
        occ.append(shifted(occ[-1], 1))
    chunks = [[(s, j) for j in range(responses)] for s in range(STEPS)]

    kernel = lookup(kernel_index, kernel_table)
    fields, done = [], []
    for s in range(STEPS):
        ready = done[-2:-1] if s else occ[1:]
        fields.append(exchange(forward(chunks[s], occ, resp, right, left), *ready))
        done.append(fields[-1])
    occ_sums, resp_sums = [None] * STEPS, [None] * responses
    order, total = [2, 3, 1, 0], None
    for i, s in enumerate(order):
        ready = done[-2:-1]
        if i > 1:
            last = order[i - 2]
            inverse(chunks[last], fields[last], occ, resp, right_scaled, left, occ_sums, resp_sums)
            ready = ready + resp_sums
        if i == 3:
            total = shifted(occ_sums[3].astype(BF), -1)
            ready.append(total)
        fields[s] = exchange(middle(fields[s], kernel, left), *ready)
        done.append(fields[s])
    total = shifted((total.astype(F32) + occ_sums[2]).astype(BF), -2)
    inverse(chunks[1], fields[1], occ, resp, right_scaled, left, occ_sums, resp_sums)
    first = shifted(occ_sums[1].astype(BF), -1)
    inverse(chunks[0], after(fields[0], total), occ, resp, right_scaled, left, occ_sums, resp_sums)
    total = occ_sums[0] + total.astype(F32) + first.astype(F32)
    return total.astype(BF), jnp.concatenate(resp_sums, axis=0).astype(BF)


def solution(mesh):
    in_specs = (
        P("band", "grid", None, None),
        P("band"),
        P("band", "grid", None, None),
        P(None, "grid", None),
        P(),
    )
    out_specs = (P("band", "grid", None, None), P("band", "grid", None, None))
    return jax.shard_map(shards, mesh=mesh, in_specs=in_specs, out_specs=out_specs, check_vma=False)
```
